32 devices in a mesh: blk: 4 (over y, x), row: 8 (over z, core).
Axes of the slice: x: 2, y: 2, z: 4, core: 2. Of those that a mesh axis runs over, the one named last changes fastest.
Arguments:
- intersection: bfloat16 [2048, 2048], P('row', 'blk'), may hold values from -0.125 to 0.125
- inverse_dev: bfloat16 [2048, 2048], P('row', 'blk'), may hold values from -0.125 to 0.125
- hamiltonian: bfloat16 [2048, 2048], P('row', 'blk'), may hold values from -0.09375 to 0.09375
- chem_potential: float32 [1], replicated, may hold values from -0.4 to 0.4
- pattern_s: int32 [16, 16], replicated, may hold values 0 or 1
- pattern_z: int32 [16, 16], replicated, may hold values 0 or 1
- pattern_h: int32 [16, 16], replicated, may hold values 0 or 1
- fill_inverse: int32 [16, 16], replicated, may hold values 0 or 1
- fill_sign: int32 [16, 16], replicated, may hold values 0 or 1
Outputs:
- refined_inverse: bfloat16 [2048, 2048], P('row', 'blk')
- inverse_error: bfloat16 [2048, 2048], P('row', 'blk')
- sign_step: bfloat16 [2048, 2048], P('row', 'blk')
The draws below stay inside these ranges and needn't reach their ends.
All inputs are finite; a program needn't handle non-finite values.
Results may differ from the reference program's by a relative error of at most 0.0067.
Values may be sent and summed in bfloat16 or wider, within the bound.
A program may use at most 64 MiB of HBM per device.

```python
import jax
import jax.numpy as jnp
from jax import lax

BS = 128
NB = 16
N = 2048


def touch_ends(entries, stream_key, smallest, high):
    place = [jax.random.randint(jax.random.fold_in(stream_key, axis), (), 0, length) for axis, length in enumerate(entries.shape)]
    widest = entries.shape.index(max(entries.shape))
    next_to = place[:widest] + [(place[widest] + 1) % entries.shape[widest]] + place[widest + 1:]
    return entries.at[tuple(place)].set(smallest).at[tuple(next_to)].set(high)


def steps_of(rng, shape, shards, low, high):
    factor_of = 1.0
    for dim, parts in shards:
        steps = jax.random.uniform(jax.random.fold_in(jax.random.fold_in(rng, 6), dim), (parts,), jnp.float32, low / len(shards), high / len(shards))
        factor_of = factor_of * jnp.repeat(jnp.exp(steps), shape[dim] // parts).reshape((-1,) + (1,) * (len(shape) - 1 - dim))
    return factor_of


def centred(own_key, shape, deviation, most, cuts=(), kind=jnp.bfloat16):
    loudness = steps_of(own_key, shape, cuts, -0.22, 0.18) if cuts else 1.0
    result = jax.random.normal(own_key, shape, jnp.float32) * deviation * loudness
    return jnp.minimum(jnp.maximum(result, -most), most).astype(kind)


def setup_inputs(seed: int = 0) -> dict:
    arg_keys = jax.random.split(jax.random.key(seed), 10)
    return {
        "intersection": centred(arg_keys[0], (N, N), N ** -0.5, 0.125, ((0, 8), (1, 4))),
        "inverse_dev": centred(arg_keys[1], (N, N), N ** -0.5, 0.125, ((0, 8), (1, 4))),
        "hamiltonian": centred(arg_keys[2], (N, N), (2 * N) ** -0.5, 0.09375, ((0, 8), (1, 4))),
        "chem_potential": jnp.clip(jax.random.uniform(arg_keys[3], (1,), jnp.float32, -0.4, 0.4), -0.4, 0.4),
        "pattern_s": touch_ends((jax.random.randint(arg_keys[4], (NB, NB), 0, 2) < 1).astype(jnp.int32), jax.random.fold_in(arg_keys[4], 1), 0, 1),
        "pattern_z": touch_ends((jax.random.randint(arg_keys[5], (NB, NB), 0, 2) < 1).astype(jnp.int32), jax.random.fold_in(arg_keys[5], 1), 0, 1),
        "pattern_h": touch_ends((jax.random.randint(arg_keys[6], (NB, NB), 0, 2) < 1).astype(jnp.int32), jax.random.fold_in(arg_keys[6], 1), 0, 1),
        "fill_inverse": touch_ends((jax.random.randint(arg_keys[7], (NB, NB), 0, 4) < 3).astype(jnp.int32), jax.random.fold_in(arg_keys[7], 1), 0, 1),
        "fill_sign": touch_ends((jax.random.randint(arg_keys[8], (NB, NB), 0, 4) < 3).astype(jnp.int32), jax.random.fold_in(arg_keys[8], 1), 0, 1),
    }


def expand(pattern):
    wide = jnp.repeat(jnp.repeat(pattern.astype(jnp.float32), BS, axis=0), BS, axis=1)
    return wide


def product(left, right):
    return jnp.dot(left.astype(jnp.float32), right.astype(jnp.float32), precision=lax.Precision.HIGHEST)


def reference(intersection, inverse_dev, hamiltonian, chem_potential, pattern_s, pattern_z, pattern_h, fill_inverse, fill_sign):
    ident = jnp.eye(N, dtype=jnp.float32)
    seff = (ident + 0.35 * expand(pattern_s) * intersection.astype(jnp.float32)).astype(jnp.bfloat16)
    zeff = (ident - 0.35 * expand(pattern_z) * inverse_dev.astype(jnp.float32)).astype(jnp.bfloat16)
    heff = (expand(pattern_h) * hamiltonian.astype(jnp.float32)).astype(jnp.bfloat16)
    first = product(zeff, seff).astype(jnp.bfloat16)
    second = product(first, zeff)
    refined = (expand(fill_inverse) * (2.0 * zeff.astype(jnp.float32) - second)).astype(jnp.bfloat16)
    error = (ident - product(refined, seff)).astype(jnp.bfloat16)
    mask_sign = expand(fill_sign)
    shifted = (mask_sign * product(refined, heff) - chem_potential[0] * ident).astype(jnp.bfloat16)
    square = (mask_sign * product(shifted, shifted)).astype(jnp.bfloat16)
    cube = product(shifted, square)
    sign = (0.5 * (3.0 * shifted.astype(jnp.float32) - cube)).astype(jnp.bfloat16)
    return refined, error, sign
```

```python
import functools

import jax
import jax.numpy as jnp
from jax import lax
from jax.experimental import pallas as pl
from jax.experimental.pallas import tpu as pltpu
from jax.sharding import PartitionSpec as P

BS = 128
MESH = pl.DeviceIdType.MESH
S, Z, H, X, Q = range(5)
ZR, FR, RR, XR = range(4)


def kernel(
    blks,
    rows_n,
    inter_ref,
    inv_ref,
    ham_ref,
    chem_ref,
    ps_ref,
    pz_ref,
    ph_ref,
    fi_ref,
    fs_ref,
    refined_ref,
    error_ref,
    sign_ref,
    cols,
    panels,
    acc,
    col_send,
    col_recv,
    row_send,
    row_recv,
):
    rows, width = inter_ref.shape
    chips = rows_n // 2
    chunk = 2 * rows
    per = width // chunk
    me_row = lax.axis_index("row")
    me_blk = lax.axis_index("blk")
    chip = me_row // 2
    core = me_row % 2
    mate = chip * 2 + (1 - core)

    def row_device(r):
        return {"row": r, "blk": me_blk}

    def blk_device(b):
        return {"row": me_row, "blk": b}

    def slot(i, r):
        return cols.at[i, pl.ds(pl.multiple_of(r * rows, rows), rows)]

    def col_copy(i, kind, c, target, source):
        return pltpu.make_async_remote_copy(
            src_ref=slot(i, source),
            dst_ref=slot(i, source),
            send_sem=col_send.at[i, kind, c],
            recv_sem=col_recv.at[i, source],
            device_id=row_device(target),
            device_id_type=MESH,
        )

    def mine(c):
        return c * 2 + core

    def up(i, c):
        return col_copy(i, 0, c, me_row + 2, mine(c))

    def down(i, c):
        return col_copy(i, 1, c, me_row - 2, mine(c))

    def across(i, c):
        return col_copy(i, 2, c, mate, mine(c))

    def from_mate(i, c):
        return col_copy(i, 2, c, mate, c * 2 + (1 - core))

    def row_copy(i, step):
        to = lax.rem(me_blk + step, blks)
        return pltpu.make_async_remote_copy(
            src_ref=panels.at[i, me_blk],
            dst_ref=panels.at[i, me_blk],
            send_sem=row_send.at[i, step],
            recv_sem=row_recv.at[i, me_blk],
            device_id=blk_device(to),
            device_id_type=MESH,
        )

    def row_arrival(i, step):
        source = lax.rem(me_blk + step, blks)
        return pltpu.make_async_remote_copy(
            src_ref=panels.at[i, source],
            dst_ref=panels.at[i, source],
            send_sem=row_send.at[i, step],
            recv_sem=row_recv.at[i, source],
            device_id=blk_device(source),
            device_id_type=MESH,
        )

    def send_rows(i):
        for step in range(1, blks):
            row_copy(i, step).start()

    def wait_rows(i):
        for step in range(1, blks):
            row_arrival(i, step).wait_recv()

    def send_own(i):
        @pl.when(chip + 1 < chips)
        def _():
            up(i, chip).start()

        @pl.when(chip > 0)
        def _():
            down(i, chip).start()

        across(i, chip).start()

    def relay(i, d):
        @pl.when(chip - d >= 0)
        def _():
            c = chip - d
            up(i, c).wait_recv()

            @pl.when(chip + 1 < chips)
            def _():
                up(i, c).start()

            across(i, c).start()

        @pl.when(chip + d < chips)
        def _():
            c = chip + d
            down(i, c).wait_recv()

            @pl.when(chip > 0)
            def _():
                down(i, c).start()

            across(i, c).start()

    def term(i, a, c):
        left = panels[a, c // per] if per == 1 else panels[a, c // per, :, pl.ds(pl.multiple_of(c % per * chunk, chunk), chunk)]
        right = cols[i, pl.ds(pl.multiple_of(c * chunk, chunk), chunk)]
        return jnp.dot(left, right, preferred_element_type=jnp.float32)

    def fold(i, a, d):
        @pl.when(chip - d >= 0)
        def _():
            c = chip - d
            from_mate(i, c).wait_recv()
            acc[...] += term(i, a, c)

        @pl.when(chip + d < chips)
        def _():
            c = chip + d
            from_mate(i, c).wait_recv()
            acc[...] += term(i, a, c)

    def loop(low, high, f):
        def step(d, carry):
            f(d)
            return carry

        lax.fori_loop(low, high, step, 0)

    def column_pass(i, a, after, fresh=True):
        loop(1, chips - 1, lambda d: relay(i, d))
        after()
        if fresh:
            wait_rows(a)
        from_mate(i, chip).wait_recv()
        acc[...] = term(i, a, chip)
        loop(1, chips - 1, lambda d: fold(i, a, d))
        if chips > 1:
            relay(i, chips - 1)
            fold(i, a, chips - 1)

    tall, wide = rows // BS, width // BS

    def tiles(f):
        for p in range(tall):
            for q in range(wide):
                f(p, q, (slice(p * BS, (p + 1) * BS), slice(q * BS, (q + 1) * BS)))

    def keep(ref, p, q):
        return ref[me_row * tall + p, me_blk * wide + q].astype(jnp.float32)

    def ident(p, q):
        gap = (me_blk * width + q * BS) - (me_row * rows + p * BS)
        i = lax.broadcasted_iota(jnp.int32, (BS, BS), 0)
        j = lax.broadcasted_iota(jnp.int32, (BS, BS), 1)
        return jnp.where(i - j == gap, 1.0, 0.0).astype(jnp.float32)

    def put_col(i, p, q, value):
        cols[
            i,
            pl.ds(pl.multiple_of(me_row * rows + p * BS, BS), BS),
            q * BS : (q + 1) * BS,
        ] = value

    def put_row(a, p, q, value):
        panels[a, me_blk, p * BS : (p + 1) * BS, q * BS : (q + 1) * BS] = value

    def make_s(p, q, at):
        value = ident(p, q) + 0.35 * keep(ps_ref, p, q) * inter_ref[at].astype(jnp.float32)
        put_col(S, p, q, value.astype(jnp.bfloat16))

    def make_z(p, q, at):
        value = ident(p, q) - 0.35 * keep(pz_ref, p, q) * inv_ref[at].astype(jnp.float32)
        value = value.astype(jnp.bfloat16)
        put_col(Z, p, q, value)
        put_row(ZR, p, q, value)

    def make_h(p, q, at):
        value = keep(ph_ref, p, q) * ham_ref[at].astype(jnp.float32)
        put_col(H, p, q, value.astype(jnp.bfloat16))

    def make_refined(p, q, at):
        own = panels[ZR, me_blk, at[0], at[1]].astype(jnp.float32)
        value = (keep(fi_ref, p, q) * (2.0 * own - acc[at])).astype(jnp.bfloat16)
        put_row(RR, p, q, value)
        refined_ref[at] = value

    def make_x(p, q, at):
        value = keep(fs_ref, p, q) * acc[at] - chem_ref[0] * ident(p, q)
        value = value.astype(jnp.bfloat16)
        put_col(X, p, q, value)
        put_row(XR, p, q, value)

    def make_q(p, q, at):
        put_col(Q, p, q, (keep(fs_ref, p, q) * acc[at]).astype(jnp.bfloat16))

    def make_error(p, q, at):
        error_ref[at] = (ident(p, q) - acc[at]).astype(jnp.bfloat16)

    def make_sign(p, q, at):
        own = panels[XR, me_blk, at[0], at[1]].astype(jnp.float32)
        sign_ref[at] = (0.5 * (3.0 * own - acc[at])).astype(jnp.bfloat16)

    barrier = pltpu.get_barrier_semaphore()

    def greet(device):
        pl.semaphore_signal(barrier, inc=1, device_id=device, device_id_type=MESH)

    greet(row_device(mate))
    for step in range(1, blks):
        greet(blk_device(lax.rem(me_blk + step, blks)))

    @pl.when(chip + 1 < chips)
    def _():
        greet(row_device(me_row + 2))

    @pl.when(chip > 0)
    def _():
        greet(row_device(me_row - 2))

    tiles(make_s)
    tiles(make_z)
    above = jnp.where(chip + 1 < chips, 1, 0)
    below = jnp.where(chip > 0, 1, 0)
    pl.semaphore_wait(barrier, blks + above + below)

    send_own(S)
    send_rows(ZR)
    tiles(make_h)

    column_pass(S, ZR, lambda: send_own(Z))
    panels[FR, me_blk] = acc[...].astype(jnp.bfloat16)
    send_rows(FR)

    column_pass(Z, FR, lambda: send_own(H))
    tiles(make_refined)
    send_rows(RR)

    column_pass(H, RR, lambda: None)
    tiles(make_x)
    send_own(X)
    send_rows(XR)

    def error_product():
        acc[...] = jnp.zeros_like(acc)

        def add(c):
            acc[...] += term(S, RR, c)

        loop(0, chips, add)
        tiles(make_error)

    column_pass(X, XR, error_product)
    tiles(make_q)
    send_own(Q)
    column_pass(Q, XR, lambda: None, fresh=False)
    tiles(make_sign)

    for i in range(5):

        def drain(c, i=i):
            @pl.when((chip + 1 < chips) & (c <= chip))
            def _():
                up(i, c).wait_send()

            @pl.when((chip > 0) & (c >= chip))
            def _():
                down(i, c).wait_send()

            across(i, c).wait_send()

        loop(0, chips, drain)
    for i in range(4):
        for step in range(1, blks):
            row_copy(i, step).wait_send()


def body(blks, rows_n, *args):
    rows, width = args[0].shape
    out = jax.ShapeDtypeStruct((rows, width), jnp.bfloat16)
    vmem = pl.BlockSpec(memory_space=pltpu.VMEM)
    smem = pl.BlockSpec(memory_space=pltpu.SMEM)
    depth = rows_n * rows
    return pl.pallas_call(
        functools.partial(kernel, blks, rows_n),
        out_shape=(out, out, out),
        in_specs=[vmem] * 3 + [smem] * 6,
        out_specs=(vmem, vmem, vmem),
        scratch_shapes=[
            pltpu.VMEM((5, depth, width), jnp.bfloat16),
            pltpu.VMEM((4, blks, rows, width), jnp.bfloat16),
            pltpu.VMEM((rows, width), jnp.float32),
            pltpu.SemaphoreType.DMA((5, 3, rows_n // 2)),
            pltpu.SemaphoreType.DMA((5, rows_n)),
            pltpu.SemaphoreType.DMA((4, blks)),
            pltpu.SemaphoreType.DMA((4, blks)),
        ],
        compiler_params=pltpu.CompilerParams(
            collective_id=0, has_side_effects=True, vmem_limit_bytes=48 * 1024 * 1024
        ),
        cost_estimate=pl.CostEstimate(
            flops=12 * rows * depth * width, bytes_accessed=12 * rows * width, transcendentals=0
        ),
    )(*args)


def solution(mesh):
    placed = (P("row", "blk"), P("row", "blk"), P("row", "blk"), P(), P(), P(), P(), P(), P())
    return jax.shard_map(
        functools.partial(body, mesh.shape["blk"], mesh.shape["row"]),
        mesh=mesh,
        in_specs=placed,
        out_specs=(P("row", "blk"), P("row", "blk"), P("row", "blk")),
        check_vma=False,
    )
```

```python
import functools

import jax
import jax.numpy as jnp
from jax import lax
from jax.experimental import pallas as pl
from jax.experimental.pallas import tpu as pltpu
from jax.sharding import PartitionSpec as P

BS = 128
PARTS = 4
MESH = pl.DeviceIdType.MESH
S, Z, H, X, Q = range(5)
ZR, FR, RR, XR = range(4)


def kernel(
    blks,
    rows_n,
    inter_hbm,
    inv_hbm,
    ham_hbm,
    chem_hbm,
    ps_hbm,
    pz_hbm,
    ph_hbm,
    fi_hbm,
    fs_hbm,
    refined_ref,
    error_ref,
    sign_ref,
    cols,
    panels,
    acc,
    col_send,
    col_recv,
    row_send,
    row_recv,
    inter_ref,
    inv_ref,
    ham_ref,
    chem_ref,
    ps_ref,
    pz_ref,
    ph_ref,
    fi_ref,
    fs_ref,
    load_sem,
):
    loads = [
        pltpu.make_async_copy(source, target, load_sem.at[n])
        for n, (source, target) in enumerate(
            (
                (inter_hbm, inter_ref),
                (ps_hbm, ps_ref),
                (inv_hbm, inv_ref),
                (pz_hbm, pz_ref),
                (ham_hbm, ham_ref),
                (ph_hbm, ph_ref),
                (fi_hbm, fi_ref),
                (fs_hbm, fs_ref),
                (chem_hbm, chem_ref),
            )
        )
    ]
    for load in loads:
        load.start()
    rows, width = inter_ref.shape
    chips = rows_n // 2
    chunk = 2 * rows
    per = width // chunk
    me_row = lax.axis_index("row")
    me_blk = lax.axis_index("blk")
    chip = me_row // 2
    core = me_row % 2
    mate = chip * 2 + (1 - core)

    def row_device(r):
        return {"row": r, "blk": me_blk}

    def blk_device(b):
        return {"row": me_row, "blk": b}

    piece = rows // PARTS

    def slot(i, r, part):
        return cols.at[i, pl.ds(pl.multiple_of(r * rows + part * piece, piece), piece)]

    def col_copy(i, kind, c, target, source, part):
        return pltpu.make_async_remote_copy(
            src_ref=slot(i, source, part),
            dst_ref=slot(i, source, part),
            send_sem=col_send.at[i, kind, c, part],
            recv_sem=col_recv.at[i, source, part],
            device_id=row_device(target),
            device_id_type=MESH,
        )

    def mine(c):
        return c * 2 + core

    def up(i, c, part):
        return col_copy(i, 0, c, me_row + 2, mine(c), part)

    def down(i, c, part):
        return col_copy(i, 1, c, me_row - 2, mine(c), part)

    def across(i, c, part):
        return col_copy(i, 2, c, mate, mine(c), part)

    def from_mate(i, c):
        for part in range(PARTS):
            col_copy(i, 2, c, mate, c * 2 + (1 - core), part).wait_recv()

    def row_copy(i, step):
        to = lax.rem(me_blk + step, blks)
        return pltpu.make_async_remote_copy(
            src_ref=panels.at[i, me_blk],
            dst_ref=panels.at[i, me_blk],
            send_sem=row_send.at[i, step],
            recv_sem=row_recv.at[i, me_blk],
            device_id=blk_device(to),
            device_id_type=MESH,
        )

    def row_arrival(i, step):
        source = lax.rem(me_blk + step, blks)
        return pltpu.make_async_remote_copy(
            src_ref=panels.at[i, source],
            dst_ref=panels.at[i, source],
            send_sem=row_send.at[i, step],
            recv_sem=row_recv.at[i, source],
            device_id=blk_device(source),
            device_id_type=MESH,
        )

    def send_rows(i):
        for step in range(1, blks):
            row_copy(i, step).start()

    def wait_rows(i):
        for step in range(1, blks):
            row_arrival(i, step).wait_recv()

    def send_own(i):
        for part in range(PARTS):

            @pl.when(chip + 1 < chips)
            def _():
                up(i, chip, part).start()

            @pl.when(chip > 0)
            def _():
                down(i, chip, part).start()

        for part in range(PARTS):
            across(i, chip, part).start()

    def relay(i, d):
        for part in range(PARTS):

            @pl.when(chip - d >= 0)
            def _():
                c = chip - d
                up(i, c, part).wait_recv()

                @pl.when(chip + 1 < chips)
                def _():
                    up(i, c, part).start()

                across(i, c, part).start()

            @pl.when(chip + d < chips)
            def _():
                c = chip + d
                down(i, c, part).wait_recv()

                @pl.when(chip > 0)
                def _():
                    down(i, c, part).start()

                across(i, c, part).start()

    def term(i, a, c):
        left = panels[a, c // per] if per == 1 else panels[a, c // per, :, pl.ds(pl.multiple_of(c % per * chunk, chunk), chunk)]
        right = cols[i, pl.ds(pl.multiple_of(c * chunk, chunk), chunk)]
        return jnp.dot(left, right, preferred_element_type=jnp.float32)

    def fold(i, a, d):
        @pl.when(chip - d >= 0)
        def _():
            c = chip - d
            from_mate(i, c)
            acc[...] += term(i, a, c)

        @pl.when(chip + d < chips)
        def _():
            c = chip + d
            from_mate(i, c)
            acc[...] += term(i, a, c)

    def loop(low, high, f):
        def step(d, carry):
            f(d)
            return carry

        lax.fori_loop(low, high, step, 0)

    def column_pass(i, a, after, fresh=True):
        loop(1, chips - 1, lambda d: relay(i, d))
        after()
        if fresh:
            wait_rows(a)
        from_mate(i, chip)
        acc[...] = term(i, a, chip)
        loop(1, chips - 1, lambda d: fold(i, a, d))
        if chips > 1:
            relay(i, chips - 1)
            fold(i, a, chips - 1)

    tall, wide = rows // BS, width // BS

    def tiles(f):
        for p in range(tall):
            for q in range(wide):
                f(p, q, (slice(p * BS, (p + 1) * BS), slice(q * BS, (q + 1) * BS)))

    def keep(ref, p, q):
        return ref[me_row * tall + p, me_blk * wide + q].astype(jnp.float32)

    def ident(p, q):
        gap = (me_blk * width + q * BS) - (me_row * rows + p * BS)
        i = lax.broadcasted_iota(jnp.int32, (BS, BS), 0)
        j = lax.broadcasted_iota(jnp.int32, (BS, BS), 1)
        return jnp.where(i - j == gap, 1.0, 0.0).astype(jnp.float32)

    def put_col(i, p, q, value):
        cols[
            i,
            pl.ds(pl.multiple_of(me_row * rows + p * BS, BS), BS),
            q * BS : (q + 1) * BS,
        ] = value

    def put_row(a, p, q, value):
        panels[a, me_blk, p * BS : (p + 1) * BS, q * BS : (q + 1) * BS] = value

    def make_s(p, q, at):
        value = ident(p, q) + 0.35 * keep(ps_ref, p, q) * inter_ref[at].astype(jnp.float32)
        put_col(S, p, q, value.astype(jnp.bfloat16))

    def make_z(p, q, at):
        value = ident(p, q) - 0.35 * keep(pz_ref, p, q) * inv_ref[at].astype(jnp.float32)
        value = value.astype(jnp.bfloat16)
        put_col(Z, p, q, value)
        put_row(ZR, p, q, value)

    def make_h(p, q, at):
        value = keep(ph_ref, p, q) * ham_ref[at].astype(jnp.float32)
        put_col(H, p, q, value.astype(jnp.bfloat16))

    def make_refined(p, q, at):
        own = panels[ZR, me_blk, at[0], at[1]].astype(jnp.float32)
        value = (keep(fi_ref, p, q) * (2.0 * own - acc[at])).astype(jnp.bfloat16)
        put_row(RR, p, q, value)
        refined_ref[at] = value

    def make_x(p, q, at):
        value = keep(fs_ref, p, q) * acc[at] - chem_ref[0] * ident(p, q)
        value = value.astype(jnp.bfloat16)
        put_col(X, p, q, value)
        put_row(XR, p, q, value)

    def make_q(p, q, at):
        put_col(Q, p, q, (keep(fs_ref, p, q) * acc[at]).astype(jnp.bfloat16))

    def make_error(p, q, at):
        error_ref[at] = (ident(p, q) - acc[at]).astype(jnp.bfloat16)

    def make_sign(p, q, at):
        own = panels[XR, me_blk, at[0], at[1]].astype(jnp.float32)
        sign_ref[at] = (0.5 * (3.0 * own - acc[at])).astype(jnp.bfloat16)

    barrier = pltpu.get_barrier_semaphore()

    def greet(device):
        pl.semaphore_signal(barrier, inc=1, device_id=device, device_id_type=MESH)

    greet(row_device(mate))
    for step in range(1, blks):
        greet(blk_device(lax.rem(me_blk + step, blks)))

    @pl.when(chip + 1 < chips)
    def _():
        greet(row_device(me_row + 2))

    @pl.when(chip > 0)
    def _():
        greet(row_device(me_row - 2))

    def arrive(first, last):
        for load in loads[first:last]:
            load.wait()

    arrive(0, 2)
    tiles(make_s)
    above = jnp.where(chip + 1 < chips, 1, 0)
    below = jnp.where(chip > 0, 1, 0)
    pl.semaphore_wait(barrier, blks + above + below)

    send_own(S)
    arrive(2, 4)
    tiles(make_z)
    send_rows(ZR)
    arrive(4, 9)
    tiles(make_h)

    column_pass(S, ZR, lambda: send_own(Z))
    panels[FR, me_blk] = acc[...].astype(jnp.bfloat16)
    send_rows(FR)

    column_pass(Z, FR, lambda: send_own(H))
    tiles(make_refined)
    send_rows(RR)

    column_pass(H, RR, lambda: None)
    tiles(make_x)
    send_own(X)
    send_rows(XR)

    def error_product():
        acc[...] = jnp.zeros_like(acc)

        def add(c):
            acc[...] += term(S, RR, c)

        loop(0, chips, add)
        tiles(make_error)

    column_pass(X, XR, error_product)
    tiles(make_q)
    send_own(Q)
    column_pass(Q, XR, lambda: None, fresh=False)
    tiles(make_sign)

    for i in range(5):

        def drain(c, i=i):
            for part in range(PARTS):

                @pl.when((chip + 1 < chips) & (c <= chip))
                def _():
                    up(i, c, part).wait_send()

                @pl.when((chip > 0) & (c >= chip))
                def _():
                    down(i, c, part).wait_send()

                across(i, c, part).wait_send()

        loop(0, chips, drain)
    for i in range(4):
        for step in range(1, blks):
            row_copy(i, step).wait_send()


def body(blks, rows_n, *args):
    rows, width = args[0].shape
    out = jax.ShapeDtypeStruct((rows, width), jnp.bfloat16)
    vmem = pl.BlockSpec(memory_space=pltpu.VMEM)
    depth = rows_n * rows
    return pl.pallas_call(
        functools.partial(kernel, blks, rows_n),
        out_shape=(out, out, out),
        in_specs=[pl.BlockSpec(memory_space=pl.ANY)] * 9,
        out_specs=(vmem, vmem, vmem),
        scratch_shapes=[
            pltpu.VMEM((5, depth, width), jnp.bfloat16),
            pltpu.VMEM((4, blks, rows, width), jnp.bfloat16),
            pltpu.VMEM((rows, width), jnp.float32),
            pltpu.SemaphoreType.DMA((5, 3, rows_n // 2, PARTS)),
            pltpu.SemaphoreType.DMA((5, rows_n, PARTS)),
            pltpu.SemaphoreType.DMA((4, blks)),
            pltpu.SemaphoreType.DMA((4, blks)),
            *(pltpu.VMEM(a.shape, a.dtype) for a in args[:3]),
            *(pltpu.SMEM(a.shape, a.dtype) for a in args[3:]),
            pltpu.SemaphoreType.DMA((9,)),
        ],
        compiler_params=pltpu.CompilerParams(
            collective_id=0, has_side_effects=True, vmem_limit_bytes=60 * 1024 * 1024
        ),
        cost_estimate=pl.CostEstimate(
            flops=12 * rows * depth * width, bytes_accessed=12 * rows * width, transcendentals=0
        ),
    )(*args)


def solution(mesh):
    placed = (P("row", "blk"), P("row", "blk"), P("row", "blk"), P(), P(), P(), P(), P(), P())
    return jax.shard_map(
        functools.partial(body, mesh.shape["blk"], mesh.shape["row"]),
        mesh=mesh,
        in_specs=placed,
        out_specs=(P("row", "blk"), P("row", "blk"), P("row", "blk")),
        check_vma=False,
    )
```

```python
import functools

import jax
import jax.numpy as jnp
from jax import lax
from jax.experimental import pallas as pl
from jax.experimental.pallas import tpu as pltpu
from jax.sharding import PartitionSpec as P

BS = 128
PARTS = 4
MESH = pl.DeviceIdType.MESH
S, Z, H, X, Q = range(5)
ZR, FR, RR, XR = range(4)


def kernel(
    blks,
    rows_n,
    inter_hbm,
    inv_hbm,
    ham_hbm,
    chem_hbm,
    ps_hbm,
    pz_hbm,
    ph_hbm,
    fi_hbm,
    fs_hbm,
    refined_ref,
    error_ref,
    sign_ref,
    cols,
    panels,
    acc,
    col_send,
    col_recv,
    row_send,
    row_recv,
    inter_ref,
    inv_ref,
    ham_ref,
    chem_ref,
    ps_ref,
    pz_ref,
    ph_ref,
    fi_ref,
    fs_ref,
    load_sem,
):
    loads = [
        pltpu.make_async_copy(source, target, load_sem.at[n])
        for n, (source, target) in enumerate(
            (
                (inter_hbm, inter_ref),
                (ps_hbm, ps_ref),
                (inv_hbm, inv_ref),
                (pz_hbm, pz_ref),
                (ham_hbm, ham_ref),
                (ph_hbm, ph_ref),
                (fi_hbm, fi_ref),
                (fs_hbm, fs_ref),
                (chem_hbm, chem_ref),
            )
        )
    ]
    for load in loads:
        load.start()
    rows, width = inter_ref.shape
    chips = rows_n // 2
    chunk = 2 * rows
    per = width // chunk
    me_row = lax.axis_index("row")
    me_blk = lax.axis_index("blk")
    chip = me_row // 2
    core = me_row % 2
    mate = chip * 2 + (1 - core)

    def row_device(r):
        return {"row": r, "blk": me_blk}

    def blk_device(b):
        return {"row": me_row, "blk": b}

    piece = rows // PARTS

    def slot(i, r, part):
        return cols.at[i, pl.ds(pl.multiple_of(r * rows + part * piece, piece), piece)]

    def col_copy(i, kind, c, target, source, part):
        return pltpu.make_async_remote_copy(
            src_ref=slot(i, source, part),
            dst_ref=slot(i, source, part),
            send_sem=col_send.at[i, kind, c, part],
            recv_sem=col_recv.at[i, source, part],
            device_id=row_device(target),
            device_id_type=MESH,
        )

    def mine(c):
        return c * 2 + core

    def up(i, c, part):
        return col_copy(i, 0, c, me_row + 2, mine(c), part)

    def down(i, c, part):
        return col_copy(i, 1, c, me_row - 2, mine(c), part)

    def across(i, c, part):
        return col_copy(i, 2, c, mate, mine(c), part)

    def from_mate(i, c):
        for part in range(PARTS):
            col_copy(i, 2, c, mate, c * 2 + (1 - core), part).wait_recv()

    def row_copy(i, step):
        to = lax.rem(me_blk + step, blks)
        return pltpu.make_async_remote_copy(
            src_ref=panels.at[i, me_blk],
            dst_ref=panels.at[i, me_blk],
            send_sem=row_send.at[i, step],
            recv_sem=row_recv.at[i, me_blk],
            device_id=blk_device(to),
            device_id_type=MESH,
        )

    def row_arrival(i, step):
        source = lax.rem(me_blk + step, blks)
        return pltpu.make_async_remote_copy(
            src_ref=panels.at[i, source],
            dst_ref=panels.at[i, source],
            send_sem=row_send.at[i, step],
            recv_sem=row_recv.at[i, source],
            device_id=blk_device(source),
            device_id_type=MESH,
        )

    def send_rows(i):
        for step in range(1, blks):
            row_copy(i, step).start()

    def wait_rows(i):
        for step in range(1, blks):
            row_arrival(i, step).wait_recv()

    def send_own(i):
        for part in range(PARTS):

            @pl.when(chip + 1 < chips)
            def _():
                up(i, chip, part).start()

            @pl.when(chip > 0)
            def _():
                down(i, chip, part).start()

        for part in range(PARTS):
            across(i, chip, part).start()

    def relay(i, d):
        for part in range(PARTS):

            @pl.when(chip - d >= 0)
            def _():
                c = chip - d
                up(i, c, part).wait_recv()

                @pl.when(chip + 1 < chips)
                def _():
                    up(i, c, part).start()

                across(i, c, part).start()

            @pl.when(chip + d < chips)
            def _():
                c = chip + d
                down(i, c, part).wait_recv()

                @pl.when(chip > 0)
                def _():
                    down(i, c, part).start()

                across(i, c, part).start()

    def term(i, a, c):
        left = panels[a, c // per] if per == 1 else panels[a, c // per, :, pl.ds(pl.multiple_of(c % per * chunk, chunk), chunk)]
        right = cols[i, pl.ds(pl.multiple_of(c * chunk, chunk), chunk)]
        return jnp.dot(left, right, preferred_element_type=jnp.float32)

    def fold(i, a, d):
        @pl.when(chip - d >= 0)
        def _():
            c = chip - d
            from_mate(i, c)
            acc[...] += term(i, a, c)

        @pl.when(chip + d < chips)
        def _():
            c = chip + d
            from_mate(i, c)
            acc[...] += term(i, a, c)

    def loop(low, high, f):
        def step(d, carry):
            f(d)
            return carry

        lax.fori_loop(low, high, step, 0)

    def column_pass(i, a, after, fresh=True):
        loop(1, chips - 1, lambda d: relay(i, d))
        after()
        if fresh:
            wait_rows(a)
        from_mate(i, chip)
        acc[...] = term(i, a, chip)
        loop(1, chips - 1, lambda d: fold(i, a, d))
        if chips > 1:
            relay(i, chips - 1)
            fold(i, a, chips - 1)

    tall, wide = rows // BS, width // BS

    def tiles(f):
        for p in range(tall):
            for q in range(wide):
                f(p, q, (slice(p * BS, (p + 1) * BS), slice(q * BS, (q + 1) * BS)))

    def keep(ref, p, q):
        return ref[me_row * tall + p, me_blk * wide + q].astype(jnp.float32)

    def ident(p, q):
        gap = (me_blk * width + q * BS) - (me_row * rows + p * BS)
        i = lax.broadcasted_iota(jnp.int32, (BS, BS), 0)
        j = lax.broadcasted_iota(jnp.int32, (BS, BS), 1)
        return jnp.where(i - j == gap, 1.0, 0.0).astype(jnp.float32)

    def put_col(i, p, q, value):
        cols[
            i,
            pl.ds(pl.multiple_of(me_row * rows + p * BS, BS), BS),
            q * BS : (q + 1) * BS,
        ] = value

    def put_row(a, p, q, value):
        panels[a, me_blk, p * BS : (p + 1) * BS, q * BS : (q + 1) * BS] = value

    def make_s(p, q, at):
        value = ident(p, q) + 0.35 * keep(ps_ref, p, q) * inter_ref[at].astype(jnp.float32)
        put_col(S, p, q, value.astype(jnp.bfloat16))

    def make_z(p, q, at):
        value = ident(p, q) - 0.35 * keep(pz_ref, p, q) * inv_ref[at].astype(jnp.float32)
        value = value.astype(jnp.bfloat16)
        put_col(Z, p, q, value)
        put_row(ZR, p, q, value)

    def make_h(p, q, at):
        value = keep(ph_ref, p, q) * ham_ref[at].astype(jnp.float32)
        put_col(H, p, q, value.astype(jnp.bfloat16))

    def make_refined(p, q, at):
        own = panels[ZR, me_blk, at[0], at[1]].astype(jnp.float32)
        value = (keep(fi_ref, p, q) * (2.0 * own - acc[at])).astype(jnp.bfloat16)
        put_row(RR, p, q, value)
        refined_ref[at] = value

    def make_x(p, q, at):
        value = keep(fs_ref, p, q) * acc[at] - chem_ref[0] * ident(p, q)
        value = value.astype(jnp.bfloat16)
        put_col(X, p, q, value)
        put_row(XR, p, q, value)

    def make_q(p, q, at):
        put_col(Q, p, q, (keep(fs_ref, p, q) * acc[at]).astype(jnp.bfloat16))

    def make_error(p, q, at):
        error_ref[at] = (ident(p, q) - acc[at]).astype(jnp.bfloat16)

    def make_sign(p, q, at):
        own = panels[XR, me_blk, at[0], at[1]].astype(jnp.float32)
        sign_ref[at] = (0.5 * (3.0 * own - acc[at])).astype(jnp.bfloat16)

    barrier = pltpu.get_barrier_semaphore()

    def greet(device):
        pl.semaphore_signal(barrier, inc=1, device_id=device, device_id_type=MESH)

    greet(row_device(mate))
    for step in range(1, blks):
        greet(blk_device(lax.rem(me_blk + step, blks)))

    @pl.when(chip + 1 < chips)
    def _():
        greet(row_device(me_row + 2))

    @pl.when(chip > 0)
    def _():
        greet(row_device(me_row - 2))

    def arrive(first, last):
        for load in loads[first:last]:
            load.wait()

    arrive(0, 2)
    tiles(make_s)
    above = jnp.where(chip + 1 < chips, 1, 0)
    below = jnp.where(chip > 0, 1, 0)
    pl.semaphore_wait(barrier, blks + above + below)

    send_own(S)
    arrive(2, 4)
    tiles(make_z)
    send_rows(ZR)
    arrive(4, 9)
    tiles(make_h)

    column_pass(S, ZR, lambda: send_own(Z))
    panels[FR, me_blk] = acc[...].astype(jnp.bfloat16)
    send_rows(FR)

    column_pass(Z, FR, lambda: send_own(H))
    tiles(make_refined)
    send_rows(RR)

    column_pass(H, RR, lambda: None)
    tiles(make_x)
    send_own(X)
    send_rows(XR)

    def error_product():
        acc[...] = jnp.zeros_like(acc)

        def add(c):
            acc[...] += term(S, RR, c)

        loop(0, chips, add)
        tiles(make_error)

    column_pass(X, XR, error_product)
    tiles(make_q)
    send_own(Q)
    column_pass(Q, XR, lambda: None, fresh=False)
    tiles(make_sign)

    for i in range(5):

        def drain(c, i=i):
            for part in range(PARTS):

                @pl.when((chip + 1 < chips) & (c <= chip))
                def _():
                    up(i, c, part).wait_send()

                @pl.when((chip > 0) & (c >= chip))
                def _():
                    down(i, c, part).wait_send()

                across(i, c, part).wait_send()

        loop(0, chips, drain)
    for i in range(4):
        for step in range(1, blks):
            row_copy(i, step).wait_send()


def hand_on(*refs):
    for source, target in zip(refs[:3], refs[3:]):
        target[...] = source[...]


def body(blks, rows_n, *args):
    rows, width = args[0].shape
    out = jax.ShapeDtypeStruct((rows, width), jnp.bfloat16)
    vmem = pl.BlockSpec(memory_space=pltpu.VMEM)
    depth = rows_n * rows
    results = pl.pallas_call(
        functools.partial(kernel, blks, rows_n),
        out_shape=(out, out, out),
        in_specs=[pl.BlockSpec(memory_space=pl.ANY)] * 9,
        out_specs=(vmem, vmem, vmem),
        scratch_shapes=[
            pltpu.VMEM((5, depth, width), jnp.bfloat16),
            pltpu.VMEM((4, blks, rows, width), jnp.bfloat16),
            pltpu.VMEM((rows, width), jnp.float32),
            pltpu.SemaphoreType.DMA((5, 3, rows_n // 2, PARTS)),
            pltpu.SemaphoreType.DMA((5, rows_n, PARTS)),
            pltpu.SemaphoreType.DMA((4, blks)),
            pltpu.SemaphoreType.DMA((4, blks)),
            *(pltpu.VMEM(a.shape, a.dtype) for a in args[:3]),
            *(pltpu.SMEM(a.shape, a.dtype) for a in args[3:]),
            pltpu.SemaphoreType.DMA((9,)),
        ],
        compiler_params=pltpu.CompilerParams(
            collective_id=0, has_side_effects=True, vmem_limit_bytes=60 * 1024 * 1024
        ),
        cost_estimate=pl.CostEstimate(
            flops=12 * rows * depth * width, bytes_accessed=12 * rows * width, transcendentals=0
        ),
    )(*args)
    return pl.pallas_call(
        hand_on,
        out_shape=(out, out, out),
        in_specs=[vmem] * 3,
        out_specs=(vmem, vmem, vmem),
    )(*results)


def solution(mesh):
    placed = (P("row", "blk"), P("row", "blk"), P("row", "blk"), P(), P(), P(), P(), P(), P())
    return jax.shard_map(
        functools.partial(body, mesh.shape["blk"], mesh.shape["row"]),
        mesh=mesh,
        in_specs=placed,
        out_specs=(P("row", "blk"), P("row", "blk"), P("row", "blk")),
        check_vma=False,
    )
```
